32 devices in a mesh: group: 2 (over x), hid: 8 (over z, y), wid: 2 (over core).
Axes of the slice: x: 2, y: 2, z: 4, core: 2. Of those that a mesh axis runs over, the one named last changes fastest.
Arguments:
- activations: bfloat16 [256, 8192], P(('group', 'hid'), 'wid'), parts along dimension 0, may hold values from -6 to 6
- gate_quant: bfloat16 [8192, 32768], P('wid', 'hid'), may hold values from -0.0625 to 0.0625
- gate_scales: float32 [64, 256], P('wid', 'hid'), may hold values from 0.5 to 2
- up_quant: bfloat16 [8192, 32768], P('wid', 'hid'), may hold values from -0.0625 to 0.0625
- up_scales: float32 [64, 256], P('wid', 'hid'), may hold values from 0.5 to 2
- down_quant: bfloat16 [32768, 8192], P('hid', 'wid'), may hold values from -0.046875 to 0.046875
- down_scales: float32 [256, 64], P('hid', 'wid'), may hold values from 0.5 to 2
Outputs:
- ffn_out: bfloat16 [256, 8192], P(('group', 'hid'), 'wid'), parts along dimension 0
The draws below stay inside these ranges and needn't reach their ends.
There are 2 independent parts, one for each index of `group`. The reference program is written for one: setup_inputs(seed, part) draws one part's arguments, and reference() takes and returns one part's arrays. A program takes and returns all parts, laid end to end along the dimension named above; an argument that names none is the same for every part. Nothing has to cross between parts.
All inputs are finite; a program needn't handle non-finite values.
Results may differ from the reference program's by a relative error of at most 0.0071.
Values may be sent and summed in bfloat16 or wider, within the bound.
No kernel may reach another device: no remote copies, remote signals or barrier semaphores. Data moves between devices by JAX's collectives and lax.ppermute only.
A program may use at most 320 MiB of HBM per device.

```python
import math
import jax
import jax.numpy as jnp

D = 8192
FF = 32768
BLOCK = 128
ROWS = 128


def raised(result, rng, source, target, shards_of, factor):
    def block_of(position):
        return (jnp.arange(result.shape[position]) // (result.shape[position] // shards_of)).reshape((-1,) + (1,) * (result.ndim - 1 - position))

    first = jax.random.permutation(rng, shards_of)[block_of(target)]
    far = (block_of(target) + shards_of // 2) % shards_of
    return jnp.where((block_of(source) == first) | (block_of(source) == far), factor * result, result)


def steps_of(stream_key, shape, split, least, high):
    def one(axis_at, parts):
        heights = jax.random.uniform(jax.random.fold_in(jax.random.fold_in(stream_key, 6), axis_at), (parts,), jnp.float32, least / len(split), high / len(split))
        return jnp.repeat(jnp.exp(heights), shape[axis_at] // parts).reshape((-1,) + (1,) * (len(shape) - axis_at - 1))

    gain = one(*split[0])
    for cut in split[1:]:
        gain = gain * one(*cut)
    return gain


def centred(key, extent, width, bound, pieces=(), held_as=jnp.bfloat16):
    level = steps_of(key, extent, pieces, -0.22, 0.18) if pieces else 1.0
    drawn = jax.random.normal(key, extent, jnp.float32) * width * level
    return jnp.minimum(jnp.maximum(drawn, -bound), bound).astype(held_as)


def heavy_noise(stream_key, shape, scale, limit, split, heavy, held_as=jnp.bfloat16):
    array = scale * jax.random.normal(stream_key, shape, jnp.float32)
    if split:
        array = array * steps_of(stream_key, shape, split, -0.22, 0.18)
    return jnp.clip(raised(array, jax.random.fold_in(stream_key, 3), *heavy), -limit, limit).astype(held_as)


def setup_inputs(seed: int = 0, part: int = 0) -> dict:
    keys = jax.random.split(jax.random.key(seed), 8)
    part_splits = jax.random.split(jax.random.fold_in(keys[7], part), 8)
    activations = centred(part_splits[0], (ROWS, D), 1.0, 6.0, ((0, 8), (1, 2)))
    gate_quant = centred(keys[1], (D, FF), D ** -0.5, 0.0625, ((0, 2), (1, 8)))
    gate_scales = jnp.clip(jnp.exp(math.log(2.0) - 1.3862944 * jax.random.uniform(keys[2], (D // BLOCK, FF // BLOCK), jnp.float32) ** steps_of(keys[2], (D // BLOCK, FF // BLOCK), ((0, 2), (1, 8)), -0.2, 0.2)), 0.5, 2.0)
    up_quant = centred(keys[3], (D, FF), D ** -0.5, 0.0625, ((0, 2), (1, 8)))
    up_scales = jnp.clip(jnp.exp(math.log(2.0) - 1.3862944 * jax.random.uniform(keys[4], (D // BLOCK, FF // BLOCK), jnp.float32) ** steps_of(keys[4], (D // BLOCK, FF // BLOCK), ((0, 2), (1, 8)), -0.2, 0.2)), 0.5, 2.0)
    down_quant = heavy_noise(keys[5], (FF, D), FF ** -0.5, 0.046875, ((0, 8), (1, 2)), (0, 1, 8, 2.0))
    down_scales = jnp.clip(jnp.exp(math.log(2.0) - 1.3862944 * jax.random.uniform(keys[6], (FF // BLOCK, D // BLOCK), jnp.float32) ** steps_of(keys[6], (FF // BLOCK, D // BLOCK), ((0, 8), (1, 2)), -0.2, 0.2)), 0.5, 2.0)
    return dict(activations=activations, gate_quant=gate_quant, gate_scales=gate_scales, up_quant=up_quant, up_scales=up_scales, down_quant=down_quant, down_scales=down_scales)


def dequantize(quant, scales):
    rows, cols = quant.shape
    blocks = quant.astype(jnp.float32).reshape(rows // BLOCK, BLOCK, cols // BLOCK, BLOCK)
    scaled = blocks * scales[:, None, :, None]
    return scaled.reshape(rows, cols).astype(jnp.bfloat16)


def reference(activations, gate_quant, gate_scales, up_quant, up_scales, down_quant, down_scales):
    gate_weight = dequantize(gate_quant, gate_scales)
    up_weight = dequantize(up_quant, up_scales)
    down_weight = dequantize(down_quant, down_scales)
    gate = jnp.dot(activations, gate_weight, preferred_element_type=jnp.float32)
    up = jnp.dot(activations, up_weight, preferred_element_type=jnp.float32)
    hidden = (jax.nn.silu(gate) * up).astype(jnp.bfloat16)
    return jnp.dot(hidden, down_weight, preferred_element_type=jnp.float32).astype(jnp.bfloat16)
```

```python
import functools

import jax
import jax.numpy as jnp
from jax import lax
from jax.experimental import pallas as pl
from jax.experimental.pallas import tpu as pltpu
from jax.sharding import PartitionSpec as P

BLOCK = 128
MIB = 1024 * 1024


def ring_order(n):
    if n % 2:
        return list(range(n))
    return list(range(0, n, 2)) + list(range(n - 1, 0, -2))


def scaled(quant_ref, scales_ref, k, col, width):
    pieces = []
    for j in range(width // BLOCK):
        block = quant_ref[k * BLOCK:(k + 1) * BLOCK, j * BLOCK:(j + 1) * BLOCK].astype(jnp.float32)
        pieces.append((block * scales_ref[k, col + j]).astype(jnp.bfloat16))
    return jnp.concatenate(pieces, axis=1) if len(pieces) > 1 else pieces[0]


def tile_dot(x_ref, quant_ref, scales_ref, col, width):
    blocks = quant_ref.shape[0] // BLOCK
    per = 2 if blocks % 2 == 0 else 1
    total = None
    for k in range(0, blocks, per):
        weight = [scaled(quant_ref, scales_ref, k + i, col, width) for i in range(per)]
        weight = jnp.concatenate(weight, axis=0) if per > 1 else weight[0]
        part = jnp.dot(x_ref[:, k * BLOCK:(k + per) * BLOCK], weight, preferred_element_type=jnp.float32)
        total = part if total is None else total + part
    return total


def gate_up_kernel(first, tile, pieces, *refs):
    xs = refs[:pieces]
    gs, us, gq, uq, g_out, u_out, send, x = refs[pieces:]
    rows = xs[0].shape[0]

    @pl.when(pl.program_id(0) == 0)
    def _():
        for i in range(pieces):
            x[i * rows:(i + 1) * rows, :] = xs[i][...]

    col = (first + pl.program_id(0)) * (tile // BLOCK)
    g = tile_dot(x, gq, gs, col, tile)
    g_out[...] = g
    send[0] = g.astype(jnp.bfloat16)
    u = tile_dot(x, uq, us, col, tile)
    u_out[...] = u
    send[1] = u.astype(jnp.bfloat16)


def gate_up(xs, gate_scales, up_scales, gate_quant, up_quant, start, chunk, tile):
    depth = gate_quant.shape[0]
    rows = xs[0].shape[0] * len(xs)
    first = start // tile
    weight_spec = pl.BlockSpec((depth, tile), lambda i: (0, first + i))
    vmem = pl.BlockSpec(memory_space=pltpu.VMEM)
    smem = pl.BlockSpec(memory_space=pltpu.SMEM)
    return pl.pallas_call(
        functools.partial(gate_up_kernel, first, tile, len(xs)),
        grid=(chunk // tile,),
        in_specs=[vmem] * len(xs) + [smem, smem, weight_spec, weight_spec],
        out_specs=[
            pl.BlockSpec((rows, tile), lambda i: (0, i)),
            pl.BlockSpec((rows, tile), lambda i: (0, i)),
            pl.BlockSpec((2, rows, tile), lambda i: (0, 0, i)),
        ],
        out_shape=[
            jax.ShapeDtypeStruct((rows, chunk), jnp.float32),
            jax.ShapeDtypeStruct((rows, chunk), jnp.float32),
            jax.ShapeDtypeStruct((2, rows, chunk), jnp.bfloat16),
        ],
        scratch_shapes=[pltpu.VMEM((rows, depth), jnp.bfloat16)],
        compiler_params=pltpu.CompilerParams(vmem_limit_bytes=48 * MIB),
        cost_estimate=pl.CostEstimate(
            flops=4 * rows * depth * chunk, bytes_accessed=4 * depth * chunk, transcendentals=0
        ),
        name="gate_up",
    )(*xs, gate_scales, up_scales, gate_quant, up_quant)


def down_kernel(first, tile, chunks, *refs):
    parts = refs[:3 * chunks]
    ds, dq, out, hidden = refs[3 * chunks:]

    @pl.when(pl.program_id(0) == 0)
    def _():
        at = 0
        for c in range(chunks):
            g_ref, u_ref, other = parts[3 * c:3 * c + 3]
            width = g_ref.shape[1]
            step = min(width, 512)
            for j in range(0, width, step):
                g = g_ref[:, j:j + step] + other[0, :, j:j + step].astype(jnp.float32)
                u = u_ref[:, j:j + step] + other[1, :, j:j + step].astype(jnp.float32)
                value = (g / (1.0 + jnp.exp(-g))) * u
                hidden[:, at + j:at + j + step] = value.astype(jnp.bfloat16)
            at += width

    col = (first + pl.program_id(0)) * (tile // BLOCK)
    out[...] = tile_dot(hidden, dq, ds, col, tile)


def down(parts, down_scales, down_quant, start, chunk, tile):
    depth = down_quant.shape[0]
    rows = parts[0].shape[0]
    first = start // tile
    vmem = pl.BlockSpec(memory_space=pltpu.VMEM)
    return pl.pallas_call(
        functools.partial(down_kernel, first, tile, len(parts) // 3),
        grid=(chunk // tile,),
        in_specs=[vmem] * len(parts)
        + [pl.BlockSpec(memory_space=pltpu.SMEM), pl.BlockSpec((depth, tile), lambda i: (0, first + i))],
        out_specs=pl.BlockSpec((rows, tile), lambda i: (0, i)),
        out_shape=jax.ShapeDtypeStruct((rows, chunk), jnp.float32),
        scratch_shapes=[pltpu.VMEM((rows, depth), jnp.bfloat16)],
        compiler_params=pltpu.CompilerParams(vmem_limit_bytes=48 * MIB),
        cost_estimate=pl.CostEstimate(
            flops=2 * rows * depth * chunk, bytes_accessed=2 * depth * chunk, transcendentals=0
        ),
        name="down",
    )(*parts, down_scales, down_quant)


def per_device(n, widths, activations, gate_quant, gate_scales, up_quant, up_scales, down_quant, down_scales):
    order = ring_order(n)
    forward = [(order[i], order[(i + 1) % n]) for i in range(n)]
    backward = [(b, a) for a, b in forward]
    ahead, behind = n // 2, n - 1 - n // 2

    blocks = [activations] + [None] * (n - 1)
    fw = bw = activations
    for step in range(1, ahead + 1):
        fw = lax.ppermute(fw, "hid", forward)
        blocks[n - step] = fw
        if step <= behind:
            bw = lax.ppermute(bw, "hid", backward)
            blocks[step] = bw

    hidden_units = gate_quant.shape[1]
    chunk = min(hidden_units, 1024)
    parts = []
    for start in range(0, hidden_units, chunk):
        g, u, send = gate_up(
            blocks, gate_scales, up_scales, gate_quant, up_quant, start, chunk, min(chunk, 256)
        )
        other = lax.ppermute(send, "wid", [(i, widths - 1 - i) for i in range(widths)])
        parts += [g, u, other]

    total = down(parts, down_scales, down_quant, 0, down_quant.shape[1], 256)

    rows = activations.shape[0]

    def mine(r):
        r = r % n
        return total[r * rows:(r + 1) * rows]

    fw, bw = mine(ahead), mine(-behind)
    for step in range(1, ahead + 1):
        got_fw = lax.ppermute(fw.astype(jnp.bfloat16), "hid", forward)
        fw = got_fw.astype(jnp.float32) + mine(ahead - step)
        if step <= behind:
            got_bw = lax.ppermute(bw.astype(jnp.bfloat16), "hid", backward)
            bw = got_bw.astype(jnp.float32)
            if step < behind:
                bw = bw + mine(step - behind)
    return ((fw + bw) if behind else fw).astype(jnp.bfloat16)


def solution(mesh):
    return jax.shard_map(
        functools.partial(per_device, mesh.shape["hid"], mesh.shape["wid"]),
        mesh=mesh,
        in_specs=(
            P(("group", "hid"), "wid"),
            P("wid", "hid"),
            P("wid", "hid"),
            P("wid", "hid"),
            P("wid", "hid"),
            P("hid", "wid"),
            P("hid", "wid"),
        ),
        out_specs=P(("group", "hid"), "wid"),
        check_vma=False,
    )
```

```python
import functools

import jax
import jax.numpy as jnp
from jax import lax
from jax.experimental import pallas as pl
from jax.experimental.pallas import tpu as pltpu
from jax.sharding import PartitionSpec as P

BLOCK = 128
MIB = 1024 * 1024
VMEM_LIMIT = 16 * MIB
VMEM = pl.BlockSpec(memory_space=pltpu.VMEM)
SMEM = pl.BlockSpec(memory_space=pltpu.SMEM)
ANY = pl.BlockSpec(memory_space=pl.ANY)


def ring_order(n):
    if n % 2:
        return list(range(n))
    return list(range(0, n, 2)) + list(range(n - 1, 0, -2))


def scaled(quant, scales_ref, k, col, width):
    pieces = []
    for j in range(width // BLOCK):
        block = quant[k * BLOCK:(k + 1) * BLOCK, j * BLOCK:(j + 1) * BLOCK]
        pieces.append((block.astype(jnp.float32) * scales_ref[k, col + j]).astype(jnp.bfloat16))
    return jnp.concatenate(pieces, axis=1) if len(pieces) > 1 else pieces[0]


def tile_dot(x_ref, quant, scales_ref, col):
    depth, width = quant.shape
    blocks = depth // BLOCK
    per = 2 if blocks % 2 == 0 else 1
    total = None
    for k in range(0, blocks, per):
        weight = [scaled(quant, scales_ref, k + i, col, width) for i in range(per)]
        weight = jnp.concatenate(weight, axis=0) if per > 1 else weight[0]
        part = jnp.dot(x_ref[:, k * BLOCK:(k + per) * BLOCK], weight, preferred_element_type=jnp.float32)
        total = part if total is None else total + part
    return total


class Tiles:
    def __init__(self, quant, buffers, sems, first, count):
        self.quant, self.buffers, self.sems = quant, buffers, sems
        self.first, self.count = first, count
        self.slots, _, self.width = buffers.shape

    def copy(self, i):
        start = (self.first + i) * self.width
        if not isinstance(i, int):
            start = pl.multiple_of(start, self.width)
        slot = lax.rem(i, self.slots)
        return pltpu.make_async_copy(
            self.quant.at[:, pl.ds(start, self.width)], self.buffers.at[slot], self.sems.at[slot]
        )

    def begin(self):
        for i in range(min(self.count, self.slots)):
            self.copy(i).start()

    def get(self, i):
        self.copy(i).wait()
        return self.buffers.at[lax.rem(i, self.slots)]

    def advance(self, i):
        @pl.when(i + self.slots < self.count)
        def _():
            self.copy(i + self.slots).start()


def tile_copies(quant, first, staged, sems):
    count, _, width = staged.shape
    return [
        pltpu.make_async_copy(
            quant.at[:, (first + i) * width:(first + i + 1) * width], staged.at[i], sems.at[i]
        )
        for i in range(count)
    ]


def in_vmem(array):
    return pltpu.with_memory_space_constraint(array, pltpu.VMEM)


def stage_kernel(first, *refs):
    quant, staged, token, sems = refs
    copies = tile_copies(quant, first, staged, sems)
    for copy in copies:
        copy.start()
    token[...] = jnp.zeros_like(token)
    for copy in copies:
        copy.wait()


def stage(quant, first, count, tile):
    depth = quant.shape[0]
    return pl.pallas_call(
        functools.partial(stage_kernel, first),
        in_specs=[ANY],
        out_specs=[VMEM, VMEM],
        out_shape=[pltpu.VMEM((count, depth, tile), quant.dtype), pltpu.VMEM((16, BLOCK), jnp.bfloat16)],
        scratch_shapes=[pltpu.SemaphoreType.DMA((count,))],
        compiler_params=pltpu.CompilerParams(vmem_limit_bytes=VMEM_LIMIT),
        cost_estimate=pl.CostEstimate(
            flops=0, bytes_accessed=2 * count * depth * tile, transcendentals=0
        ),
        name="stage",
    )(quant)


def gate_up_kernel(first, tiles, places, keep_x, stage_next, *refs):
    refs = list(refs)
    xs = [refs.pop(0) for _ in places]
    gs, us, gq, uq, _ = [refs.pop(0) for _ in range(5)]
    dq = refs.pop(0) if stage_next else None
    own, send = refs.pop(0), refs.pop(0)
    x = refs.pop(0) if keep_x else xs[0]
    staged = refs.pop(0) if stage_next else None
    buffers, sems, staged_sems = refs
    tile = gq.shape[2]
    ups = Tiles(uq, buffers, sems, first, tiles)
    ups.begin()
    if keep_x:
        for ref, (row, col) in zip(xs, places):
            x[row:row + ref.shape[0], col:col + ref.shape[1]] = ref[...]
    copies = tile_copies(dq, 0, staged, staged_sems) if stage_next else []

    @pl.loop(0, tiles)
    def _(i):
        col = (first + i) * (tile // BLOCK)
        g = tile_dot(x, gq.at[first + i], gs, col)
        own[0, i] = g
        send[0, i] = g.astype(jnp.bfloat16)
        u = tile_dot(x, ups.get(i), us, col)
        own[1, i] = u
        send[1, i] = u.astype(jnp.bfloat16)
        ups.advance(i)

        @pl.when(i == max(tiles - ups.slots, 1) - 1)
        def _():
            for copy in copies:
                copy.start()

    for copy in copies:
        copy.wait()


def gate_up(xs, places, rows, gate_scales, up_scales, gate_tiles, up_quant, first, end, slots, down_quant, stage_next, token):
    _, depth, tile = gate_tiles.shape
    tiles = end - first
    keep_x = len(xs) > 1
    out_shape = [
        pltpu.VMEM((2, tiles, rows, tile), jnp.float32),
        jax.ShapeDtypeStruct((2, tiles, rows, tile), jnp.bfloat16),
    ]
    if keep_x:
        out_shape.append(pltpu.VMEM((rows, depth), jnp.bfloat16))
    if stage_next:
        out_shape.append(pltpu.VMEM((stage_next, down_quant.shape[0], tile), down_quant.dtype))
    return pl.pallas_call(
        functools.partial(gate_up_kernel, first, tiles, places[:len(xs)], keep_x, stage_next),
        in_specs=[VMEM] * len(xs) + [SMEM, SMEM, VMEM, ANY, ANY] + [ANY] * (stage_next > 0),
        out_specs=[VMEM] * len(out_shape),
        out_shape=out_shape,
        scratch_shapes=[
            pltpu.VMEM((slots, depth, tile), jnp.bfloat16),
            pltpu.SemaphoreType.DMA((slots,)),
            pltpu.SemaphoreType.DMA((max(stage_next, 1),)),
        ],
        compiler_params=pltpu.CompilerParams(
            vmem_limit_bytes=max(VMEM_LIMIT, slots * depth * tile * 2 + 3 * rows * depth + 3 * MIB)
        ),
        cost_estimate=pl.CostEstimate(
            flops=4 * rows * depth * tile * tiles, bytes_accessed=4 * depth * tile * tiles, transcendentals=0
        ),
        name="gate_up",
    )(*xs, gate_scales, up_scales, in_vmem(gate_tiles), up_quant, token, *([down_quant] if stage_next else []))


def down_kernel(parts_of, *refs):
    refs = list(refs)
    parts = [(refs.pop(0), refs.pop(0)) for _ in range(parts_of)]
    ds, resident, dq, out, hidden, buffers, sems = refs
    kept, _, tile = resident.shape
    tiles = out.shape[0]
    downs = Tiles(dq, buffers, sems, kept, tiles - kept)
    downs.begin()
    at = 0
    for own, other in parts:
        for i in range(own.shape[1]):
            g = own[0, i] + other[0, i].astype(jnp.float32)
            u = own[1, i] + other[1, i].astype(jnp.float32)
            width = own.shape[3]
            hidden[:, at:at + width] = ((g / (1.0 + jnp.exp(-g))) * u).astype(jnp.bfloat16)
            at += width

    @pl.loop(0, kept)
    def _(i):
        out[i] = tile_dot(hidden, resident.at[i], ds, i * (tile // BLOCK))

    @pl.loop(0, tiles - kept)
    def _(i):
        out[kept + i] = tile_dot(hidden, downs.get(i), ds, (kept + i) * (tile // BLOCK))
        downs.advance(i)


def down(parts, down_scales, resident, down_quant, slots):
    depth, width = down_quant.shape
    tile = resident.shape[2]
    rows = parts[0].shape[2]
    return pl.pallas_call(
        functools.partial(down_kernel, len(parts) // 2),
        in_specs=[VMEM] * len(parts) + [SMEM, VMEM, ANY],
        out_specs=VMEM,
        out_shape=pltpu.VMEM((width // tile, rows, tile), jnp.float32),
        scratch_shapes=[
            pltpu.VMEM((rows, depth), jnp.bfloat16),
            pltpu.VMEM((slots, depth, tile), jnp.bfloat16),
            pltpu.SemaphoreType.DMA((slots,)),
        ],
        compiler_params=pltpu.CompilerParams(
            vmem_limit_bytes=max(VMEM_LIMIT, slots * depth * tile * 2 + 14 * rows * depth - 4 * MIB)
        ),
        cost_estimate=pl.CostEstimate(
            flops=2 * rows * depth * width, bytes_accessed=2 * depth * width, transcendentals=0
        ),
        name="down",
    )(*parts, down_scales, in_vmem(resident), down_quant)


def gather_rows(own, n, shift, beside):
    rows, width = own.shape
    if n == 8:
        half = width // 2
        two_back, two_ahead = shift(own, 2), shift(own, -2)
        one_back, one_ahead = shift(own, 1), shift(own, -1)
        two_back, two_ahead, beside = lax.optimization_barrier((two_back, two_ahead, beside))
        three_back, three_ahead = shift(two_back, 1), shift(two_ahead, -1)
        left, right = shift(two_back[:, :half], 2), shift(two_ahead[:, half:], -2)
        blocks = [own, one_ahead, two_ahead, three_ahead, left, right, three_back, two_back, one_back]
        at = [0, 1, 2, 3, 4, 4, 5, 6, 7]
        return blocks, [(r * rows, half if i == 5 else 0) for i, r in enumerate(at)], beside
    blocks = [own] + [None] * (n - 1)
    fw = bw = own
    for step in range(1, n // 2 + 1):
        fw = shift(fw, 1)
        blocks[n - step] = fw
        if step <= n - 1 - n // 2:
            bw = shift(bw, -1)
            blocks[step] = bw
    return [jnp.concatenate(blocks, axis=0)], [(0, 0)], beside


def scatter_sums(total, n, rows, shift):
    def mine(r):
        r = r % n
        return total[:, r * rows:(r + 1) * rows]

    def sent(value, by):
        return shift(value.astype(jnp.bfloat16), by).astype(jnp.float32)

    if n == 8:
        half = total.shape[0] // 2
        far_left, far_right = sent(mine(4)[:half], 2), sent(mine(4)[half:], -2)
        third, fifth = sent(mine(3), 1), sent(mine(5), -1)
        first, last = sent(mine(1), 1), sent(mine(7), -1)
        ahead, behind = mine(2) + third, mine(6) + fifth
        ahead = jnp.concatenate([ahead[:half] + far_left, ahead[half:]], axis=0)
        behind = jnp.concatenate([behind[:half], behind[half:] + far_right], axis=0)
        return mine(0) + first + last + sent(ahead, 2) + sent(behind, -2)
    ahead, behind = n // 2, n - 1 - n // 2
    fw, bw = mine(ahead), mine(-behind)
    for step in range(1, ahead + 1):
        fw = sent(fw, 1) + mine(ahead - step)
        if step <= behind:
            bw = sent(bw, -1)
            if step < behind:
                bw = bw + mine(step - behind)
    return (fw + bw) if behind else fw


def per_device(n, widths, activations, gate_quant, gate_scales, up_quant, up_scales, down_quant, down_scales):
    order = ring_order(n)

    def shift(value, by):
        return lax.ppermute(value, "hid", [(order[i], order[(i + by) % n]) for i in range(n)])

    rows = activations.shape[0]
    gate_quant, up_quant, down_quant = (
        pltpu.with_memory_space_constraint(a, pltpu.HBM) for a in (gate_quant, up_quant, down_quant)
    )
    hidden_units, width = gate_quant.shape[1], down_quant.shape[1]
    tile = min(hidden_units, 512)
    tiles = hidden_units // tile
    cuts = [0, tiles // 2, tiles] if tiles > 2 else [0, tiles]
    gate_tiles, token = stage(gate_quant, 0, tiles, tile)
    xs, places, token = gather_rows(activations, n, shift, token)
    parts = []
    for start, end in zip(cuts[:-1], cuts[1:]):
        stage_next = min(2, width // tile) if end == tiles else 0
        outs = gate_up(
            xs, places, n * rows, gate_scales, up_scales, gate_tiles, up_quant, start, end, 2, down_quant, stage_next, token
        )
        if len(xs) > 1:
            xs = [outs[2]]
        other = lax.ppermute(outs[1], "wid", [(i, widths - 1 - i) for i in range(widths)])
        parts += [outs[0], other]
    total = down(parts, down_scales, outs[-1], down_quant, 3)
    result = scatter_sums(total, n, rows, shift).astype(jnp.bfloat16)
    return result.transpose(1, 0, 2).reshape(rows, width)


def solution(mesh):
    return jax.shard_map(
        functools.partial(per_device, mesh.shape["hid"], mesh.shape["wid"]),
        mesh=mesh,
        in_specs=(
            P(("group", "hid"), "wid"),
            P("wid", "hid"),
            P("wid", "hid"),
            P("wid", "hid"),
            P("wid", "hid"),
            P("hid", "wid"),
            P("hid", "wid"),
        ),
        out_specs=P(("group", "hid"), "wid"),
        check_vma=False,
    )
```

```python
import functools

import jax
import jax.numpy as jnp
from jax import lax
from jax.experimental import pallas as pl
from jax.experimental.pallas import tpu as pltpu
from jax.sharding import PartitionSpec as P

BLOCK = 128
MIB = 1024 * 1024
VMEM_LIMIT = 16 * MIB
KEPT = 2
VMEM = pl.BlockSpec(memory_space=pltpu.VMEM)
SMEM = pl.BlockSpec(memory_space=pltpu.SMEM)
ANY = pl.BlockSpec(memory_space=pl.ANY)


def ring_order(n):
    if n % 2:
        return list(range(n))
    return list(range(0, n, 2)) + list(range(n - 1, 0, -2))


def scaled(quant, scales_ref, k, col, width):
    pieces = []
    for j in range(width // BLOCK):
        block = quant[k * BLOCK:(k + 1) * BLOCK, j * BLOCK:(j + 1) * BLOCK]
        pieces.append((block.astype(jnp.float32) * scales_ref[k, col + j]).astype(jnp.bfloat16))
    return jnp.concatenate(pieces, axis=1) if len(pieces) > 1 else pieces[0]


def tile_dot(x_ref, quant, scales_ref, col):
    depth, width = quant.shape
    blocks = depth // BLOCK
    per = 2 if blocks % 2 == 0 else 1
    total = None
    for k in range(0, blocks, per):
        weight = [scaled(quant, scales_ref, k + i, col, width) for i in range(per)]
        weight = jnp.concatenate(weight, axis=0) if per > 1 else weight[0]
        part = jnp.dot(x_ref[:, k * BLOCK:(k + per) * BLOCK], weight, preferred_element_type=jnp.float32)
        total = part if total is None else total + part
    return total


class Tiles:
    def __init__(self, quant, buffers, sems, first, count):
        self.quant, self.buffers, self.sems = quant, buffers, sems
        self.first, self.count = first, count
        self.slots, _, self.width = buffers.shape

    def copy(self, i):
        start = (self.first + i) * self.width
        if not isinstance(i, int):
            start = pl.multiple_of(start, self.width)
        slot = lax.rem(i, self.slots)
        return pltpu.make_async_copy(
            self.quant.at[:, pl.ds(start, self.width)], self.buffers.at[slot], self.sems.at[slot]
        )

    def start(self, i):
        if isinstance(i, int):
            if i < min(self.count, self.slots):
                self.copy(i).start()
            return

        @pl.when(i < min(self.count, self.slots))
        def _():
            self.copy(i).start()

    def get(self, i):
        self.copy(i).wait()
        return self.buffers.at[lax.rem(i, self.slots)]

    def advance(self, i):
        @pl.when(i + self.slots < self.count)
        def _():
            self.copy(i + self.slots).start()


def tile_copies(quant, first, staged, at, count, sems):
    width = staged.shape[2]
    return [
        pltpu.make_async_copy(
            quant.at[:, (first + i) * width:(first + i + 1) * width], staged.at[at + i], sems.at[i]
        )
        for i in range(count)
    ]


def in_vmem(array):
    return pltpu.with_memory_space_constraint(array, pltpu.VMEM)


def stage_kernel(first, at, count, *refs):
    quant, staged, token, sems = refs[0], refs[-3], refs[-2], refs[-1]
    copies = tile_copies(quant, first, staged, at, count, sems)
    for copy in copies:
        copy.start()
    token[...] = jnp.zeros_like(token)
    for copy in copies:
        copy.wait()


def stage(quant, first, tile, total, at, count, filled=None, after=()):
    depth = quant.shape[0]
    more = list(after) if filled is None else [in_vmem(filled), *after]
    return pl.pallas_call(
        functools.partial(stage_kernel, first, at, count),
        in_specs=[ANY] + ([] if filled is None else [VMEM]) + [ANY] * len(after),
        out_specs=[VMEM, VMEM],
        out_shape=[pltpu.VMEM((total, depth, tile), quant.dtype), pltpu.VMEM((16, BLOCK), jnp.bfloat16)],
        input_output_aliases={} if filled is None else {1: 0},
        scratch_shapes=[pltpu.SemaphoreType.DMA((count,))],
        compiler_params=pltpu.CompilerParams(vmem_limit_bytes=VMEM_LIMIT),
        cost_estimate=pl.CostEstimate(
            flops=0, bytes_accessed=2 * count * depth * tile, transcendentals=0
        ),
        name="stage",
    )(quant, *more)


def gate_up_kernel(first, tiles, places, keep_x, *refs):
    refs = list(refs)
    xs = [refs.pop(0) for _ in places]
    gs, us, gq, uq, _ = [refs.pop(0) for _ in range(5)]
    own, send = refs.pop(0), refs.pop(0)
    x = refs.pop(0) if keep_x else xs[0]
    buffers, sems = refs
    tile = gq.shape[2]
    ups = Tiles(uq, buffers, sems, first, tiles)
    ups.start(0)
    if keep_x:
        for ref, (row, col) in zip(xs, places):
            x[row:row + ref.shape[0], col:col + ref.shape[1]] = ref[...]

    def gate(i):
        g = tile_dot(x, gq.at[first + i], gs, (first + i) * (tile // BLOCK))
        own[0, i] = g
        send[0, i] = g.astype(jnp.bfloat16)

    def up(i):
        u = tile_dot(x, ups.get(i), us, (first + i) * (tile // BLOCK))
        own[1, i] = u
        send[1, i] = u.astype(jnp.bfloat16)
        ups.advance(i)

    lead = min(ups.slots, tiles)

    @pl.loop(0, tiles + lead)
    def _(i):
        @pl.when(i >= lead)
        def _():
            up(i - lead)

        @pl.when(i < tiles)
        def _():
            gate(i)

        @pl.when(i < lead)
        def _():
            ups.start(i + 1)


def gate_up(xs, places, rows, gate_scales, up_scales, gate_tiles, up_quant, first, end, slots, token):
    _, depth, tile = gate_tiles.shape
    tiles = end - first
    keep_x = len(xs) > 1
    out_shape = [
        pltpu.VMEM((2, tiles, rows, tile), jnp.float32),
        jax.ShapeDtypeStruct((2, tiles, rows, tile), jnp.bfloat16),
    ]
    if keep_x:
        out_shape.append(pltpu.VMEM((rows, depth), jnp.bfloat16))
    return pl.pallas_call(
        functools.partial(gate_up_kernel, first, tiles, places[:len(xs)], keep_x),
        in_specs=[VMEM] * len(xs) + [SMEM, SMEM, VMEM, ANY, ANY],
        out_specs=[VMEM] * len(out_shape),
        out_shape=out_shape,
        scratch_shapes=[
            pltpu.VMEM((slots, depth, tile), jnp.bfloat16),
            pltpu.SemaphoreType.DMA((slots,)),
        ],
        compiler_params=pltpu.CompilerParams(
            vmem_limit_bytes=max(VMEM_LIMIT, slots * depth * tile * 2 + 3 * rows * depth + 3 * MIB)
        ),
        cost_estimate=pl.CostEstimate(
            flops=4 * rows * depth * tile * tiles, bytes_accessed=4 * depth * tile * tiles, transcendentals=0
        ),
        name="gate_up",
    )(*xs, gate_scales, up_scales, in_vmem(gate_tiles), up_quant, token)


def activate(parts, hidden, at):
    for own, other in parts:
        width = own.shape[3]
        for i in range(own.shape[1]):
            g = own[0, i] + other[0, i].astype(jnp.float32)
            u = own[1, i] + other[1, i].astype(jnp.float32)
            hidden[:, at:at + width] = ((g / (1.0 + jnp.exp(-g))) * u).astype(jnp.bfloat16)
            at += width


def prepare_kernel(parts_of, *refs):
    refs = list(refs)
    quant = refs.pop(0)
    parts = [(refs.pop(0), refs.pop(0)) for _ in range(parts_of)]
    staged, hidden, sems = refs[-3:]
    copies = tile_copies(quant, 0, staged, 0, staged.shape[0], sems)
    for copy in copies:
        copy.start()
    activate(parts, hidden, 0)
    for copy in copies:
        copy.wait()


def prepare(down_quant, parts, tile, kept, after):
    depth = down_quant.shape[0]
    rows = parts[0].shape[2]
    units = sum(own.shape[1] * own.shape[3] for own in parts[::2])
    return pl.pallas_call(
        functools.partial(prepare_kernel, len(parts) // 2),
        in_specs=[ANY] + [VMEM] * len(parts) + [ANY],
        out_specs=[VMEM, VMEM],
        out_shape=[
            pltpu.VMEM((kept, depth, tile), down_quant.dtype),
            pltpu.VMEM((rows, units), jnp.bfloat16),
        ],
        scratch_shapes=[pltpu.SemaphoreType.DMA((kept,))],
        compiler_params=pltpu.CompilerParams(vmem_limit_bytes=VMEM_LIMIT),
        cost_estimate=pl.CostEstimate(
            flops=0, bytes_accessed=2 * kept * depth * tile, transcendentals=rows * units
        ),
        name="prepare",
    )(down_quant, *parts, after)


def down_kernel(*refs):
    early, own, other, ds, resident, dq, out, hidden, buffers, sems = refs
    kept, _, tile = resident.shape
    tiles = out.shape[0]
    downs = Tiles(dq, buffers, sems, kept, tiles - kept)
    downs.start(0)
    units = early.shape[1]
    hidden[:, :units] = early[...]
    activate([(own, other)], hidden, units)
    downs.start(1)

    @pl.loop(0, kept)
    def _(i):
        out[i] = tile_dot(hidden, resident.at[i], ds, i * (tile // BLOCK))
        downs.start(i + 2)

    for i in range(kept + 2, downs.slots):
        downs.start(i)

    @pl.loop(0, tiles - kept)
    def _(i):
        out[kept + i] = tile_dot(hidden, downs.get(i), ds, (kept + i) * (tile // BLOCK))
        downs.advance(i)


def down(early, own, other, down_scales, resident, down_quant, slots):
    depth, width = down_quant.shape
    tile = resident.shape[2]
    rows = own.shape[2]
    return pl.pallas_call(
        down_kernel,
        in_specs=[VMEM, VMEM, VMEM, SMEM, VMEM, ANY],
        out_specs=VMEM,
        out_shape=pltpu.VMEM((width // tile, rows, tile), jnp.float32),
        scratch_shapes=[
            pltpu.VMEM((rows, depth), jnp.bfloat16),
            pltpu.VMEM((slots, depth, tile), jnp.bfloat16),
            pltpu.SemaphoreType.DMA((slots,)),
        ],
        compiler_params=pltpu.CompilerParams(
            vmem_limit_bytes=max(VMEM_LIMIT, slots * depth * tile * 2 + 14 * rows * depth - 4 * MIB)
        ),
        cost_estimate=pl.CostEstimate(
            flops=2 * rows * depth * width, bytes_accessed=2 * depth * width, transcendentals=0
        ),
        name="down",
    )(early, own, other, down_scales, in_vmem(resident), down_quant)


def gather_rows(own, n, shift, beside):
    rows, width = own.shape
    if n == 8:
        half = width // 2
        two_back, two_ahead = shift(own, 2), shift(own, -2)
        one_back, one_ahead = shift(own, 1), shift(own, -1)
        two_back, two_ahead, beside = lax.optimization_barrier((two_back, two_ahead, beside))
        three_back, three_ahead = shift(two_back, 1), shift(two_ahead, -1)
        left, right = shift(two_back[:, :half], 2), shift(two_ahead[:, half:], -2)
        blocks = [own, one_ahead, two_ahead, three_ahead, left, right, three_back, two_back, one_back]
        at = [0, 1, 2, 3, 4, 4, 5, 6, 7]
        return blocks, [(r * rows, half if i == 5 else 0) for i, r in enumerate(at)], beside, (two_back,)
    blocks = [own] + [None] * (n - 1)
    fw = bw = own
    for step in range(1, n // 2 + 1):
        fw = shift(fw, 1)
        blocks[n - step] = fw
        if step <= n - 1 - n // 2:
            bw = shift(bw, -1)
            blocks[step] = bw
    return [jnp.concatenate(blocks, axis=0)], [(0, 0)], beside, ()


def scatter_sums(total, n, rows, shift):
    def mine(r):
        r = r % n
        return total[:, r * rows:(r + 1) * rows]

    def sent(value, by):
        return shift(value.astype(jnp.bfloat16), by).astype(jnp.float32)

    if n == 8:
        half = total.shape[0] // 2
        far_left, far_right = sent(mine(4)[:half], 2), sent(mine(4)[half:], -2)
        third, fifth = sent(mine(3), 1), sent(mine(5), -1)
        first, last = sent(mine(1), 1), sent(mine(7), -1)
        ahead, behind = mine(2) + third, mine(6) + fifth
        ahead = jnp.concatenate([ahead[:half] + far_left, ahead[half:]], axis=0)
        behind = jnp.concatenate([behind[:half], behind[half:] + far_right], axis=0)
        return mine(0) + first + last + sent(ahead, 2) + sent(behind, -2)
    ahead, behind = n // 2, n - 1 - n // 2
    fw, bw = mine(ahead), mine(-behind)
    for step in range(1, ahead + 1):
        fw = sent(fw, 1) + mine(ahead - step)
        if step <= behind:
            bw = sent(bw, -1)
            if step < behind:
                bw = bw + mine(step - behind)
    return (fw + bw) if behind else fw


def per_device(n, widths, activations, gate_quant, gate_scales, up_quant, up_scales, down_quant, down_scales):
    order = ring_order(n)

    def shift(value, by):
        return lax.ppermute(value, "hid", [(order[i], order[(i + by) % n]) for i in range(n)])

    rows = activations.shape[0]
    gate_quant, up_quant, down_quant = (
        pltpu.with_memory_space_constraint(a, pltpu.HBM) for a in (gate_quant, up_quant, down_quant)
    )
    hidden_units, width = gate_quant.shape[1], down_quant.shape[1]
    tile = min(hidden_units // 2, 512)
    tiles = hidden_units // tile
    cuts = [0, tiles * 3 // 4, tiles]
    early = tiles * 3 // 4
    gate_tiles, token = stage(gate_quant, 0, tile, tiles, 0, early)
    xs, places, token, second = gather_rows(activations, n, shift, token)
    if early < tiles:
        gate_tiles, token = stage(gate_quant, early, tile, tiles, early, tiles - early, gate_tiles, (token, *second))
    parts = []
    for start, end in zip(cuts[:-1], cuts[1:]):
        outs = gate_up(
            xs, places, n * rows, gate_scales, up_scales, gate_tiles, up_quant, start, end, 2, token
        )
        if len(xs) > 1:
            xs = [outs[2]]
        other = lax.ppermute(outs[1], "wid", [(i, widths - 1 - i) for i in range(widths)])
        parts += [outs[0], other]
    resident, hidden = prepare(down_quant, parts[:-2], tile, min(KEPT, width // tile), outs[0])
    total = down(hidden, *parts[-2:], down_scales, resident, down_quant, 3)
    result = scatter_sums(total, n, rows, shift).astype(jnp.bfloat16)
    return result.transpose(1, 0, 2).reshape(rows, width)


def solution(mesh):
    return jax.shard_map(
        functools.partial(per_device, mesh.shape["hid"], mesh.shape["wid"]),
        mesh=mesh,
        in_specs=(
            P(("group", "hid"), "wid"),
            P("wid", "hid"),
            P("wid", "hid"),
            P("wid", "hid"),
            P("wid", "hid"),
            P("hid", "wid"),
            P("hid", "wid"),
        ),
        out_specs=P(("group", "hid"), "wid"),
        check_vma=False,
    )
```

```python
import functools

import jax
import jax.numpy as jnp
from jax import lax
from jax.experimental import pallas as pl
from jax.experimental.pallas import tpu as pltpu
from jax.sharding import PartitionSpec as P

BLOCK = 128
MIB = 1024 * 1024
VMEM = pl.BlockSpec(memory_space=pltpu.VMEM)
SMEM = pl.BlockSpec(memory_space=pltpu.SMEM)
ANY = pl.BlockSpec(memory_space=pl.ANY)


def ring_order(n):
    if n % 2:
        return list(range(n))
    return list(range(0, n, 2)) + list(range(n - 1, 0, -2))


def scaled(quant, scales_ref, k, row, col, width):
    pieces = []
    for j in range(width // BLOCK):
        block = quant[k * BLOCK:(k + 1) * BLOCK, j * BLOCK:(j + 1) * BLOCK]
        pieces.append((block.astype(jnp.float32) * scales_ref[row + k, col + j]).astype(jnp.bfloat16))
    return jnp.concatenate(pieces, axis=1) if len(pieces) > 1 else pieces[0]


def tile_dot(x_ref, quant, scales_ref, row, col):
    depth, width = quant.shape
    blocks = depth // BLOCK
    per = 2 if blocks % 2 == 0 else 1
    total = None
    for k in range(0, blocks, per):
        weight = [scaled(quant, scales_ref, k + i, row, col, width) for i in range(per)]
        weight = jnp.concatenate(weight, axis=0) if per > 1 else weight[0]
        part = jnp.dot(x_ref[:, k * BLOCK:(k + per) * BLOCK], weight, preferred_element_type=jnp.float32)
        total = part if total is None else total + part
    return total


def tile_copy(quant, i, store, slot, sem):
    depth, width = quant.shape[0], store.shape[2]
    start = i * width if isinstance(i, int) else pl.multiple_of(i * width, width)
    return pltpu.make_async_copy(quant.at[:, pl.ds(start, width)], store.at[slot, pl.ds(0, depth)], sem)


def in_vmem(array):
    return pltpu.with_memory_space_constraint(array, pltpu.VMEM)


def limit(rows, depth):
    return pltpu.CompilerParams(vmem_limit_bytes=max(13 * MIB, 6 * MIB + 4 * rows * depth))


def stage_kernel(first, count, *refs):
    quant, store, token, sems = refs[0], refs[-3], refs[-2], refs[-1]
    copies = [tile_copy(quant, first + i, store, first + i, sems.at[i]) for i in range(count)]
    for copy in copies:
        copy.start()
    token[...] = jnp.zeros_like(token)
    for copy in copies:
        copy.wait()


def stage(quant, tile, count, rows, slots):
    depth = quant.shape[0]
    return pl.pallas_call(
        functools.partial(stage_kernel, 0, count),
        in_specs=[ANY],
        out_specs=[VMEM, VMEM],
        out_shape=[pltpu.VMEM((slots, depth, tile), quant.dtype), pltpu.VMEM((16, BLOCK), jnp.bfloat16)],
        scratch_shapes=[pltpu.SemaphoreType.DMA((count,))],
        compiler_params=limit(rows, depth),
        cost_estimate=pl.CostEstimate(
            flops=0, bytes_accessed=2 * count * depth * tile, transcendentals=0
        ),
        name="stage",
    )(quant)


def gate_up_kernel(first, tiles, gate_at, spare, rest, places, downs, *refs):
    refs = list(refs)
    xs = [refs.pop(0) for _ in places]
    scales, _, uq, nq, _ = [refs.pop(0) for _ in range(5)]
    store, own, send = refs.pop(0), refs.pop(0), refs.pop(0)
    x = refs.pop(0) if len(places) > 1 else xs[0]
    sems, next_sems = refs
    tile = store.shape[2]
    blocks = scales.shape[0] // 2

    def slot_of(i):
        return jnp.where(i < 2, spare + i, i - 2)

    def up_copy(i):
        return tile_copy(uq, first + i, store, slot_of(i), sems.at[i])

    copies = [(0, tile_copy(nq, i, store, i, next_sems.at[i])) for i in range(downs)]
    for i in range(rest):
        at = tiles - rest + i
        copies.append((at, tile_copy(nq, first + tiles + i, store, at, next_sems.at[i])))
        copies.append((tiles + i, tile_copy(uq, first + tiles + i, store, spare + i, next_sems.at[rest + i])))
    if rest:
        for i in range(min(2, tiles)):
            up_copy(jnp.int32(i)).start()
    if len(places) > 1:
        for ref, (row, col) in zip(xs, places):
            x[row:row + ref.shape[0], col:col + ref.shape[1]] = ref[...]

    @pl.loop(0, 2 * tiles)
    def _(step):
        part = jnp.where(step < tiles, 0, 1)
        i = step - part * tiles
        slot = jnp.where(step < tiles, gate_at + i, slot_of(i))

        if rest:
            @pl.when(step >= tiles)
            def _():
                up_copy(i).wait()

        value = tile_dot(x, store.at[slot], scales, part * blocks, (first + i) * (tile // BLOCK))
        own[part, i] = value
        send[part, i] = value.astype(jnp.bfloat16)

        if rest:
            @pl.when(step + 2 < tiles)
            def _():
                up_copy(step + 2).start()

        for at, copy in copies:
            pl.when(step == at)(copy.start)

    for _, copy in copies:
        copy.wait()


def gate_up(xs, places, rows, scales, store, up_quant, next_quant, first, end, gate_at, spare, rest, downs, token):
    slots, depth, tile = store.shape
    tiles = end - first
    out_shape = [
        pltpu.VMEM(store.shape, store.dtype),
        pltpu.VMEM((2, tiles, rows, tile), jnp.float32),
        jax.ShapeDtypeStruct((2, tiles, rows, tile), jnp.bfloat16),
    ]
    if len(xs) > 1:
        out_shape.append(pltpu.VMEM((rows, depth), jnp.bfloat16))
    return pl.pallas_call(
        functools.partial(gate_up_kernel, first, tiles, gate_at, spare, rest, places[:len(xs)], downs),
        in_specs=[VMEM] * len(xs) + [SMEM, VMEM, ANY, ANY, ANY],
        out_specs=[VMEM] * len(out_shape),
        out_shape=out_shape,
        input_output_aliases={len(xs) + 1: 0},
        scratch_shapes=[
            pltpu.SemaphoreType.DMA((tiles,)),
            pltpu.SemaphoreType.DMA((max(downs, 2 * rest, 1),)),
        ],
        compiler_params=limit(rows, depth),
        cost_estimate=pl.CostEstimate(
            flops=4 * rows * depth * tile * tiles, bytes_accessed=4 * depth * tile * tiles, transcendentals=0
        ),
        name="gate_up",
    )(*xs, scales, in_vmem(store), up_quant, next_quant, token)


def activate(own, other, hidden, at):
    width = own.shape[3]
    for i in range(own.shape[1]):
        g = own[0, i] + other[0, i].astype(jnp.float32)
        u = own[1, i] + other[1, i].astype(jnp.float32)
        hidden[:, at:at + width] = ((g / (1.0 + jnp.exp(-g))) * u).astype(jnp.bfloat16)
        at += width


def prepare_kernel(downs, kept, dq, own, other, _, after, store, hidden, sems):
    copies = [tile_copy(dq, downs + i, store, downs + i, sems.at[i]) for i in range(kept)]
    for copy in copies:
        copy.start()
    activate(own, other, hidden, 0)
    for copy in copies:
        copy.wait()


def prepare(down_quant, own, other, store, downs, kept, after):
    rows, units = own.shape[2], own.shape[1] * own.shape[3]
    tile = store.shape[2]
    return pl.pallas_call(
        functools.partial(prepare_kernel, downs, kept),
        in_specs=[ANY, VMEM, VMEM, VMEM, ANY],
        out_specs=[VMEM, VMEM],
        out_shape=[pltpu.VMEM(store.shape, store.dtype), pltpu.VMEM((rows, units), jnp.bfloat16)],
        input_output_aliases={3: 0},
        scratch_shapes=[pltpu.SemaphoreType.DMA((kept,))],
        compiler_params=limit(rows, store.shape[1]),
        cost_estimate=pl.CostEstimate(
            flops=0, bytes_accessed=2 * kept * down_quant.shape[0] * tile, transcendentals=rows * units
        ),
        name="prepare",
    )(down_quant, own, other, in_vmem(store), after)


def down_kernel(kept, early, own, other, scales, _, dq, store, out, hidden, sems):
    slots, _, tile = store.shape
    tiles, depth = out.shape[0], dq.shape[0]

    def copy(i):
        return tile_copy(dq, i, store, lax.rem(i, slots), sems.at[lax.rem(i, slots)])

    for i in range(kept, min(kept + 2, tiles)):
        copy(jnp.int32(i)).start()
    units = early.shape[1]
    hidden[:, :units] = early[...]
    activate(own, other, hidden, units)

    @pl.loop(0, tiles)
    def _(i):
        @pl.when(i >= kept)
        def _():
            copy(i).wait()

        quant = store.at[lax.rem(i, slots), pl.ds(0, depth)]
        out[i] = tile_dot(hidden, quant, scales, 0, i * (tile // BLOCK))

        @pl.when(i + kept + 2 < tiles)
        def _():
            copy(i + kept + 2).start()


def down(early, own, other, scales, store, down_quant, kept):
    depth, width = down_quant.shape
    slots, _, tile = store.shape
    rows = own.shape[2]
    return pl.pallas_call(
        functools.partial(down_kernel, kept),
        in_specs=[VMEM, VMEM, VMEM, SMEM, VMEM, ANY],
        out_specs=[VMEM, VMEM],
        out_shape=[
            pltpu.VMEM(store.shape, store.dtype),
            pltpu.VMEM((width // tile, rows, tile), jnp.float32),
        ],
        input_output_aliases={4: 0},
        scratch_shapes=[pltpu.VMEM((rows, depth), jnp.bfloat16), pltpu.SemaphoreType.DMA((slots,))],
        compiler_params=limit(rows, store.shape[1]),
        cost_estimate=pl.CostEstimate(
            flops=2 * rows * depth * width, bytes_accessed=2 * depth * width, transcendentals=0
        ),
        name="down",
    )(early, own, other, scales, in_vmem(store), down_quant)[1]


def gather_rows(own, n, shift, beside):
    rows, width = own.shape
    if n == 8:
        half = width // 2
        two_back, two_ahead = shift(own, 2), shift(own, -2)
        one_back, one_ahead = shift(own, 1), shift(own, -1)
        two_back, two_ahead, beside = lax.optimization_barrier((two_back, two_ahead, beside))
        three_back, three_ahead = shift(two_back, 1), shift(two_ahead, -1)
        left, right = shift(two_back[:, :half], 2), shift(two_ahead[:, half:], -2)
        blocks = [own, one_ahead, two_ahead, three_ahead, left, right, three_back, two_back, one_back]
        at = [0, 1, 2, 3, 4, 4, 5, 6, 7]
        return blocks, [(r * rows, half if i == 5 else 0) for i, r in enumerate(at)], beside
    blocks = [own] + [None] * (n - 1)
    fw = bw = own
    for step in range(1, n // 2 + 1):
        fw = shift(fw, 1)
        blocks[n - step] = fw
        if step <= n - 1 - n // 2:
            bw = shift(bw, -1)
            blocks[step] = bw
    return [jnp.concatenate(blocks, axis=0)], [(0, 0)], beside


def scatter_sums(total, n, rows, shift):
    def mine(r):
        r = r % n
        return total[:, r * rows:(r + 1) * rows]

    def sent(value, by):
        return shift(value.astype(jnp.bfloat16), by).astype(jnp.float32)

    if n == 8:
        half = total.shape[0] // 2
        far_right, far_left = sent(mine(4)[half:], -2), sent(mine(4)[:half], 2)
        fifth, third = sent(mine(5), -1), sent(mine(3), 1)
        last, first = sent(mine(7), -1), sent(mine(1), 1)
        behind, ahead = mine(6) + fifth, mine(2) + third
        behind = jnp.concatenate([behind[:half], behind[half:] + far_right], axis=0)
        ahead = jnp.concatenate([ahead[:half] + far_left, ahead[half:]], axis=0)
        return mine(0) + last + first + sent(behind, -2) + sent(ahead, 2)
    ahead, behind = n // 2, n - 1 - n // 2
    fw, bw = mine(ahead), mine(-behind)
    for step in range(1, ahead + 1):
        fw = sent(fw, 1) + mine(ahead - step)
        if step <= behind:
            bw = sent(bw, -1)
            if step < behind:
                bw = bw + mine(step - behind)
    return (fw + bw) if behind else fw


def per_device(n, widths, activations, gate_quant, gate_scales, up_quant, up_scales, down_quant, down_scales):
    order = ring_order(n)

    def shift(value, by):
        return lax.ppermute(value, "hid", [(order[i], order[(i + by) % n]) for i in range(n)])

    rows = activations.shape[0]
    gate_quant, up_quant, down_quant = (
        pltpu.with_memory_space_constraint(a, pltpu.HBM) for a in (gate_quant, up_quant, down_quant)
    )
    hidden_units, width = gate_quant.shape[1], down_quant.shape[1]
    tile = min(hidden_units // 2, 512)
    tiles = hidden_units // tile
    early = tiles * 3 // 4
    rest, slots = tiles - early, early + 2
    scales = jnp.concatenate([gate_scales, up_scales], axis=0)
    store, token = stage(gate_quant, tile, early, n * rows, slots)
    xs, places, token = gather_rows(activations, n, shift, token)
    downs = min(2, early - rest)
    parts = []
    for start, end, at, more, ahead in ((0, early, 0, rest, 0), (early, tiles, early - rest, 0, downs)):
        store, own, send, *kept_x = gate_up(
            xs, places, n * rows, scales, store, up_quant, down_quant if start else gate_quant,
            start, end, at, early, more, ahead, token,
        )
        xs = kept_x or xs
        parts.append((own, lax.ppermute(send, "wid", [(i, widths - 1 - i) for i in range(widths)])))
    more = min(2, slots - 2 - downs)
    store, hidden = prepare(down_quant, *parts[0], store, downs, more, parts[1][0])
    total = down(hidden, *parts[1], down_scales, store, down_quant, downs + more)
    result = scatter_sums(total, n, rows, shift).astype(jnp.bfloat16)
    return result.transpose(1, 0, 2).reshape(rows, width)


def solution(mesh):
    return jax.shard_map(
        functools.partial(per_device, mesh.shape["hid"], mesh.shape["wid"]),
        mesh=mesh,
        in_specs=(
            P(("group", "hid"), "wid"),
            P("wid", "hid"),
            P("wid", "hid"),
            P("wid", "hid"),
            P("wid", "hid"),
            P("hid", "wid"),
            P("hid", "wid"),
        ),
        out_specs=P(("group", "hid"), "wid"),
        check_vma=False,
    )
```

```python
import functools

import jax
import jax.numpy as jnp
from jax import lax
from jax.experimental import pallas as pl
from jax.experimental.pallas import tpu as pltpu
from jax.sharding import PartitionSpec as P

BLOCK = 128
MIB = 1024 * 1024
VMEM = pl.BlockSpec(memory_space=pltpu.VMEM)
SMEM = pl.BlockSpec(memory_space=pltpu.SMEM)
ANY = pl.BlockSpec(memory_space=pl.ANY)


def ring_order(n):
    if n % 2:
        return list(range(n))
    return list(range(0, n, 2)) + list(range(n - 1, 0, -2))


def scaled(quant, scales_ref, k, row, col, width):
    pieces = []
    for j in range(width // BLOCK):
        block = quant[k * BLOCK:(k + 1) * BLOCK, j * BLOCK:(j + 1) * BLOCK]
        pieces.append((block.astype(jnp.float32) * scales_ref[row + k, col + j]).astype(jnp.bfloat16))
    return jnp.concatenate(pieces, axis=1) if len(pieces) > 1 else pieces[0]


def tile_dot(x_ref, quant, scales_ref, row, col):
    depth, width = quant.shape
    blocks = depth // BLOCK
    per = 2 if blocks % 2 == 0 else 1
    total = None
    for k in range(0, blocks, per):
        weight = [scaled(quant, scales_ref, k + i, row, col, width) for i in range(per)]
        weight = jnp.concatenate(weight, axis=0) if per > 1 else weight[0]
        part = jnp.dot(x_ref[:, k * BLOCK:(k + per) * BLOCK], weight, preferred_element_type=jnp.float32)
        total = part if total is None else total + part
    return total


def tile_copy(quant, i, store, slot, sem):
    depth, width = quant.shape[0], store.shape[2]
    start = i * width if isinstance(i, int) else pl.multiple_of(i * width, width)
    return pltpu.make_async_copy(quant.at[:, pl.ds(start, width)], store.at[slot, pl.ds(0, depth)], sem)


def in_vmem(array):
    return pltpu.with_memory_space_constraint(array, pltpu.VMEM)


def limit(rows, depth):
    return pltpu.CompilerParams(vmem_limit_bytes=max(13 * MIB, 6 * MIB + 4 * rows * depth))


def stage_kernel(count, slot, *refs):
    quant, store, token, sems = refs[0], refs[-3], refs[-2], refs[-1]
    copies = [tile_copy(quant, i, store, slot + i, sems.at[i]) for i in range(count)]
    for copy in copies:
        copy.start()
    token[...] = jnp.zeros_like(token)
    for copy in copies:
        copy.wait()


def stage(quant, tile, count, rows, slot, shape=None, store=None, after=()):
    depth = quant.shape[0]
    more = list(after) if store is None else [in_vmem(store), *after]
    shape = shape or store.shape
    return pl.pallas_call(
        functools.partial(stage_kernel, count, slot),
        in_specs=[ANY] + ([] if store is None else [VMEM]) + [ANY] * len(after),
        out_specs=[VMEM, VMEM],
        out_shape=[pltpu.VMEM(shape, quant.dtype), pltpu.VMEM((16, BLOCK), jnp.bfloat16)],
        input_output_aliases={} if store is None else {1: 0},
        scratch_shapes=[pltpu.SemaphoreType.DMA((count,))],
        compiler_params=limit(rows, depth),
        cost_estimate=pl.CostEstimate(
            flops=0, bytes_accessed=2 * count * depth * tile, transcendentals=0
        ),
        name="stage",
    )(quant, *more)


def gate_up_kernel(first, tiles, gate_at, spare, rest, places, downs, *refs):
    refs = list(refs)
    xs = [refs.pop(0) for _ in places]
    scales, _, uq, nq, _ = [refs.pop(0) for _ in range(5)]
    store, own, send = refs.pop(0), refs.pop(0), refs.pop(0)
    x = refs.pop(0) if len(places) > 1 else xs[0]
    sems, next_sems = refs
    tile = store.shape[2]
    blocks = scales.shape[0] // 2

    def slot_of(i):
        return jnp.where(i < 2, spare + i, i - 2)

    def up_copy(i):
        return tile_copy(uq, first + i, store, slot_of(i), sems.at[i])

    copies = [(0, tile_copy(nq, i, store, i, next_sems.at[i])) for i in range(downs)]
    for i in range(rest):
        at = tiles - rest + i
        copies.append((at, tile_copy(nq, first + tiles + i, store, at, next_sems.at[i])))
        copies.append((tiles + i, tile_copy(uq, first + tiles + i, store, spare + i, next_sems.at[rest + i])))
    if len(places) > 1:
        for ref, (row, col) in zip(xs, places):
            x[row:row + ref.shape[0], col:col + ref.shape[1]] = ref[...]

    @pl.loop(0, 2 * tiles)
    def _(step):
        part = jnp.where(step < tiles, 0, 1)
        i = step - part * tiles
        slot = jnp.where(step < tiles, gate_at + i, slot_of(i))

        if rest:
            @pl.when(step >= tiles + 2)
            def _():
                up_copy(i).wait()

        value = tile_dot(x, store.at[slot], scales, part * blocks, (first + i) * (tile // BLOCK))
        own[part, i] = value
        send[part, i] = value.astype(jnp.bfloat16)

        if rest:
            @pl.when(step + 2 < tiles)
            def _():
                up_copy(step + 2).start()

        for at, copy in copies:
            pl.when(step == at)(copy.start)

    for _, copy in copies:
        copy.wait()


def gate_up(xs, places, rows, scales, store, up_quant, next_quant, first, end, gate_at, spare, rest, downs, token):
    slots, depth, tile = store.shape
    tiles = end - first
    out_shape = [
        pltpu.VMEM(store.shape, store.dtype),
        pltpu.VMEM((2, tiles, rows, tile), jnp.float32),
        jax.ShapeDtypeStruct((2, tiles, rows, tile), jnp.bfloat16),
    ]
    if len(xs) > 1:
        out_shape.append(pltpu.VMEM((rows, depth), jnp.bfloat16))
    return pl.pallas_call(
        functools.partial(gate_up_kernel, first, tiles, gate_at, spare, rest, places[:len(xs)], downs),
        in_specs=[VMEM] * len(xs) + [SMEM, VMEM, ANY, ANY, ANY],
        out_specs=[VMEM] * len(out_shape),
        out_shape=out_shape,
        input_output_aliases={len(xs) + 1: 0},
        scratch_shapes=[
            pltpu.SemaphoreType.DMA((tiles,)),
            pltpu.SemaphoreType.DMA((max(downs, 2 * rest, 1),)),
        ],
        compiler_params=limit(rows, depth),
        cost_estimate=pl.CostEstimate(
            flops=4 * rows * depth * tile * tiles, bytes_accessed=4 * depth * tile * tiles, transcendentals=0
        ),
        name="gate_up",
    )(*xs, scales, in_vmem(store), up_quant, next_quant, token)


def activate(own, other, hidden, at):
    width = own.shape[3]
    for i in range(own.shape[1]):
        g = own[0, i] + other[0, i].astype(jnp.float32)
        u = own[1, i] + other[1, i].astype(jnp.float32)
        hidden[:, at:at + width] = ((g / (1.0 + jnp.exp(-g))) * u).astype(jnp.bfloat16)
        at += width


def prepare_kernel(downs, kept, dq, own, other, _, after, store, hidden, sems):
    copies = [tile_copy(dq, downs + i, store, downs + i, sems.at[i]) for i in range(kept)]
    for copy in copies:
        copy.start()
    activate(own, other, hidden, 0)
    for copy in copies:
        copy.wait()


def prepare(down_quant, own, other, store, downs, kept, after):
    rows, units = own.shape[2], own.shape[1] * own.shape[3]
    tile = store.shape[2]
    return pl.pallas_call(
        functools.partial(prepare_kernel, downs, kept),
        in_specs=[ANY, VMEM, VMEM, VMEM, ANY],
        out_specs=[VMEM, VMEM],
        out_shape=[pltpu.VMEM(store.shape, store.dtype), pltpu.VMEM((rows, units), jnp.bfloat16)],
        input_output_aliases={3: 0},
        scratch_shapes=[pltpu.SemaphoreType.DMA((kept,))],
        compiler_params=limit(rows, store.shape[1]),
        cost_estimate=pl.CostEstimate(
            flops=0, bytes_accessed=2 * kept * down_quant.shape[0] * tile, transcendentals=rows * units
        ),
        name="prepare",
    )(down_quant, own, other, in_vmem(store), after)


def down_kernel(kept, early, own, other, scales, _, dq, store, out, hidden, sems):
    slots, _, tile = store.shape
    tiles, depth = out.shape[0], dq.shape[0]

    def copy(i):
        return tile_copy(dq, i, store, lax.rem(i, slots), sems.at[lax.rem(i, slots)])

    for i in range(kept, min(kept + 2, tiles)):
        copy(jnp.int32(i)).start()
    units = early.shape[1]
    hidden[:, :units] = early[...]
    activate(own, other, hidden, units)

    @pl.loop(0, tiles)
    def _(i):
        @pl.when(i >= kept)
        def _():
            copy(i).wait()

        quant = store.at[lax.rem(i, slots), pl.ds(0, depth)]
        out[i] = tile_dot(hidden, quant, scales, 0, i * (tile // BLOCK))

        @pl.when(i + kept + 2 < tiles)
        def _():
            copy(i + kept + 2).start()


def down(early, own, other, scales, store, down_quant, kept):
    depth, width = down_quant.shape
    slots, _, tile = store.shape
    rows = own.shape[2]
    return pl.pallas_call(
        functools.partial(down_kernel, kept),
        in_specs=[VMEM, VMEM, VMEM, SMEM, VMEM, ANY],
        out_specs=[VMEM, VMEM],
        out_shape=[
            pltpu.VMEM(store.shape, store.dtype),
            pltpu.VMEM((width // tile, rows, tile), jnp.float32),
        ],
        input_output_aliases={4: 0},
        scratch_shapes=[pltpu.VMEM((rows, depth), jnp.bfloat16), pltpu.SemaphoreType.DMA((slots,))],
        compiler_params=limit(rows, store.shape[1]),
        cost_estimate=pl.CostEstimate(
            flops=2 * rows * depth * width, bytes_accessed=2 * depth * width, transcendentals=0
        ),
        name="down",
    )(early, own, other, scales, in_vmem(store), down_quant)[1]


def gather_rows(own, n, shift, beside):
    rows, width = own.shape
    if n == 8:
        half = width // 2
        two_back, two_ahead = shift(own, 2), shift(own, -2)
        one_back, one_ahead = shift(own, 1), shift(own, -1)
        two_back, two_ahead, beside = lax.optimization_barrier((two_back, two_ahead, beside))
        three_back, three_ahead = shift(two_back, 1), shift(two_ahead, -1)
        left, right = shift(two_back[:, :half], 2), shift(two_ahead[:, half:], -2)
        blocks = [own, one_ahead, two_ahead, three_ahead, left, right, three_back, two_back, one_back]
        at = [0, 1, 2, 3, 4, 4, 5, 6, 7]
        return blocks, [(r * rows, half if i == 5 else 0) for i, r in enumerate(at)], beside, (two_back,)
    blocks = [own] + [None] * (n - 1)
    fw = bw = own
    for step in range(1, n // 2 + 1):
        fw = shift(fw, 1)
        blocks[n - step] = fw
        if step <= n - 1 - n // 2:
            bw = shift(bw, -1)
            blocks[step] = bw
    return [jnp.concatenate(blocks, axis=0)], [(0, 0)], beside, ()


def scatter_sums(total, n, rows, shift):
    def mine(r):
        r = r % n
        return total[:, r * rows:(r + 1) * rows]

    def sent(value, by):
        return shift(value.astype(jnp.bfloat16), by).astype(jnp.float32)

    if n == 8:
        half = total.shape[0] // 2
        far_right, far_left = sent(mine(4)[half:], -2), sent(mine(4)[:half], 2)
        fifth, third = sent(mine(5), -1), sent(mine(3), 1)
        last, first = sent(mine(7), -1), sent(mine(1), 1)
        behind, ahead = mine(6) + fifth, mine(2) + third
        behind = jnp.concatenate([behind[:half], behind[half:] + far_right], axis=0)
        ahead = jnp.concatenate([ahead[:half] + far_left, ahead[half:]], axis=0)
        return mine(0) + last + first + sent(behind, -2) + sent(ahead, 2)
    ahead, behind = n // 2, n - 1 - n // 2
    fw, bw = mine(ahead), mine(-behind)
    for step in range(1, ahead + 1):
        fw = sent(fw, 1) + mine(ahead - step)
        if step <= behind:
            bw = sent(bw, -1)
            if step < behind:
                bw = bw + mine(step - behind)
    return (fw + bw) if behind else fw


def per_device(n, widths, activations, gate_quant, gate_scales, up_quant, up_scales, down_quant, down_scales):
    order = ring_order(n)

    def shift(value, by):
        return lax.ppermute(value, "hid", [(order[i], order[(i + by) % n]) for i in range(n)])

    rows = activations.shape[0]
    gate_quant, up_quant, down_quant = (
        pltpu.with_memory_space_constraint(a, pltpu.HBM) for a in (gate_quant, up_quant, down_quant)
    )
    hidden_units, width = gate_quant.shape[1], down_quant.shape[1]
    tile = min(hidden_units // 2, 512)
    tiles = hidden_units // tile
    early = tiles * 3 // 4
    rest, slots = tiles - early, early + 2
    scales = jnp.concatenate([gate_scales, up_scales], axis=0)
    store, token = stage(gate_quant, tile, early, n * rows, 0, (slots, gate_quant.shape[0], tile))
    xs, places, token, second = gather_rows(activations, n, shift, token)
    store, token = stage(up_quant, tile, min(2, early), n * rows, early, store=store, after=(token, *second))
    downs = min(2, early - rest)
    parts = []
    for start, end, at, more, ahead in ((0, early, 0, rest, 0), (early, tiles, early - rest, 0, downs)):
        store, own, send, *kept_x = gate_up(
            xs, places, n * rows, scales, store, up_quant, down_quant if start else gate_quant,
            start, end, at, early, more, ahead, token,
        )
        xs = kept_x or xs
        parts.append((own, lax.ppermute(send, "wid", [(i, widths - 1 - i) for i in range(widths)])))
    more = min(2, slots - 2 - downs)
    store, hidden = prepare(down_quant, *parts[0], store, downs, more, parts[1][0])
    total = down(hidden, *parts[1], down_scales, store, down_quant, downs + more)
    result = scatter_sums(total, n, rows, shift).astype(jnp.bfloat16)
    return result.transpose(1, 0, 2).reshape(rows, width)


def solution(mesh):
    return jax.shard_map(
        functools.partial(per_device, mesh.shape["hid"], mesh.shape["wid"]),
        mesh=mesh,
        in_specs=(
            P(("group", "hid"), "wid"),
            P("wid", "hid"),
            P("wid", "hid"),
            P("wid", "hid"),
            P("wid", "hid"),
            P("hid", "wid"),
            P("hid", "wid"),
        ),
        out_specs=P(("group", "hid"), "wid"),
        check_vma=False,
    )
```
